512 devices in a mesh: orb: 64 (over x, z), aux: 8 (over y, core).
Axes of the slice: x: 4, y: 4, z: 16, core: 2. Of those that a mesh axis runs over, the one named last changes fastest.
Arguments:
- three_centre: float32 [128, 2, 64, 32768], P('orb', None, None, 'aux'), may hold values from -9 to 9, as said below
- green_occ: float32 [128, 2, 4096], P('orb'), may hold values from -2 to 2, as said below
- green_virt: float32 [128, 2, 4096], P('orb'), may hold values from -2 to 2, as said below
- owned_counts: int32 [64], replicated, may hold values from 1 to 2, 96 in all
- pattern: int32 [128, 3], P('orb'), may hold values 0 or 1
Outputs:
- chi: float32 [512, 512], P('aux', 'orb')
The draws below stay inside these ranges and needn't reach their ends.
Inputs may be any that keep to these rules, and one draw needn't show every extreme that they name: `owned_counts`: the counts sum to 96. For every row r and auxiliary function P, the diagonal block with entries three_centre[r, 0, k, P * 64 + j] is symmetric in k and j. Every diagonal block green_occ[r, 0] is symmetric. Every diagonal block green_virt[r, 0] is symmetric.
All inputs are finite; a program needn't handle non-finite values. No bound on the sum of `pattern` on one device may be relied on, other than what follows from the above.
Results may differ from the reference program's by a relative error of at most 0.0003.
Values sent between devices are 32-bit elements; how exact they have to be, the bound alone decides.
A program may use at most 128 MiB of HBM per device.

```python
import math
import jax
import jax.numpy as jnp
import numpy as np
from jax import lax

BS = 64
AUX = 512
CAP = 2
NB = 96
N_ORB = 64


half_root = 0.7071067811865476


def symmetric_blocks(key, lead_shape, bound):
    raw = jax.random.truncated_normal(key, -bound, bound, lead_shape + (BS, BS), jnp.float32)
    return (raw + jnp.swapaxes(raw, -1, -2)) * half_root


def draw_three_centre(key, part):
    rows = N_ORB * CAP
    diag_key = jax.random.fold_in(key, 11)
    upper_key = jax.random.fold_in(key, 12)
    diagonal = symmetric_blocks(diag_key, (rows, AUX), 6.0)
    diagonal = jnp.transpose(diagonal, (0, 2, 1, 3)).reshape(rows, BS, AUX * BS)
    upper = jax.random.truncated_normal(upper_key, -6.0, 6.0, (rows, BS, AUX * BS), jnp.float32)
    return jnp.stack([diagonal, upper], axis=1)


def green_blocks(key):
    rows = N_ORB * CAP
    scale = (3.0 * BS) ** (-0.5)
    diag_key = jax.random.fold_in(key, 21)
    upper_key = jax.random.fold_in(key, 22)
    diagonal = symmetric_blocks(diag_key, (rows,), 4.0).reshape(rows, BS * BS) * scale
    upper = jax.random.truncated_normal(upper_key, -4.0, 4.0, (rows, BS * BS), jnp.float32) * scale
    return jnp.stack([diagonal, upper], axis=1)


def draw_green_occ(key, part):
    return green_blocks(jax.random.fold_in(key, 31))


def draw_green_virt(key, part):
    return green_blocks(jax.random.fold_in(key, 32))


def touch_ends(values, own_key, smallest, high):
    spot = [jax.random.randint(jax.random.fold_in(own_key, axis), (), 0, length) for axis, length in enumerate(values.shape)]
    widest = values.shape.index(max(values.shape))
    neighbour = spot[:widest] + [(spot[widest] + 1) % values.shape[widest]] + spot[widest + 1:]
    return values.at[tuple(spot)].set(smallest).at[tuple(neighbour)].set(high)


def profile(count, total, limit, slope):
    weights = [(1 << 20) // math.isqrt(rank ** slope) + 1 for rank in range(2, count + 1)]
    surplus, given = total - limit - (count - 1), [1] * (count - 1)
    while surplus > 0:
        movable = [i for i in range(count - 1) if given[i] < limit]
        whole, left = sum([weights[i] for i in movable]), surplus
        for i in movable:
            more = min(limit - given[i], max(1, left * weights[i] // whole), surplus)
            given[i] = given[i] + more
            surplus = surplus - more
    return np.array([limit] + given)


def uneven_parts(key, count, total, reach, skew):
    if count == 2:
        one = jax.random.randint(key, (), max(1, total - reach), min(reach, total - 1) + 1)
        return jnp.stack([one, total - one])
    lengths = jnp.asarray(profile(count, total, reach, skew), jnp.int32)
    pairs = (count - 1) // 2
    source_of, sink = lengths[1:1 + 2 * pairs:2], lengths[2:2 + 2 * pairs:2]
    margin = jnp.minimum(source_of - 1, reach - sink)
    passed = jax.random.randint(jax.random.fold_in(key, 1), (pairs,), 0, 1 << 20) % (margin + 1)
    lengths = lengths.at[1:1 + 2 * pairs:2].set(source_of - passed).at[2:2 + 2 * pairs:2].set(sink + passed)
    return lengths[jax.random.permutation(jax.random.fold_in(key, 2), count)]


def setup_inputs(seed: int = 0) -> dict:
    streams_of = jax.random.split(jax.random.key(seed), 6)
    three_centre = draw_three_centre(jax.random.fold_in(streams_of[5], 71), 0)
    green_occ = draw_green_occ(jax.random.fold_in(streams_of[5], 71), 0)
    green_virt = draw_green_virt(jax.random.fold_in(streams_of[5], 71), 0)
    owned_counts = uneven_parts(streams_of[3], N_ORB, NB, CAP, 2).astype(jnp.int32)
    pattern = touch_ends((jax.random.randint(streams_of[4], (N_ORB * CAP, 3), 0, 4) < 3).astype(jnp.int32), jax.random.fold_in(streams_of[4], 1), 0, 1)
    return {"three_centre": three_centre, "green_occ": green_occ, "green_virt": green_virt, "owned_counts": owned_counts, "pattern": pattern}


HIGHEST = lax.Precision.HIGHEST

def contract(subscripts, first_operand, second_operand):
    return jnp.einsum(subscripts, first_operand, second_operand, precision=HIGHEST, preferred_element_type=jnp.float32)

def chain_layout(owned_counts):
    block_ends = jnp.cumsum(owned_counts)
    starts = block_ends - owned_counts
    positions = jnp.arange(NB, dtype=jnp.int32)
    owners = lax.optimization_barrier(jnp.sum((positions[:, None] >= block_ends[None, :]).astype(jnp.int32), axis=1)).astype(jnp.int32)
    return (owners * CAP + positions - starts[owners]).astype(jnp.int32)

def tensor_block(wide_block):
    return jnp.transpose(wide_block.reshape(BS, AUX, BS), (1, 0, 2))

def reference(three_centre, green_occ, green_virt, owned_counts, pattern):
    chain_rows = chain_layout(owned_counts)

    def fetch(position):
        inside = jnp.logical_and(position >= 0, position < NB)
        clipped = jnp.clip(position, 0, NB - 1).astype(jnp.int32)
        slot_row = chain_rows[clipped]
        block_live = inside.astype(jnp.float32)
        upper_ok = jnp.logical_and(inside, position < NB - 1).astype(jnp.int32)
        upper_live = (pattern[slot_row] * upper_ok).astype(jnp.float32)
        tensor_pair = three_centre[slot_row]
        diag_b = tensor_block(tensor_pair[0]) * block_live
        upper_b = tensor_block(tensor_pair[1]) * upper_live[0]
        diag_o = green_occ[slot_row, 0].reshape(BS, BS) * block_live
        upper_o = green_occ[slot_row, 1].reshape(BS, BS) * upper_live[1]
        diag_v = green_virt[slot_row, 0].reshape(BS, BS) * block_live
        upper_v = green_virt[slot_row, 1].reshape(BS, BS) * upper_live[2]
        return (diag_b, upper_b, diag_o, upper_o, diag_v, upper_v)

    def row_step(running, position):
        prev_b, prev_u, prev_do, prev_uo, prev_dv, prev_uv = fetch(position - 1)
        cur_b, cur_u, cur_do, cur_uo, cur_dv, cur_uv = fetch(position)
        next_b, next_u, next_do, next_uo, next_dv, next_uv = fetch(position + 1)
        occ_left = contract('ik,pjk->pij', cur_do, prev_u) + contract('ki,pkj->pij', prev_uo, prev_b)
        occ_mid = contract('ki,pkj->pij', prev_uo, prev_u) + contract('ik,pkj->pij', cur_do, cur_b) + contract('ik,pjk->pij', cur_uo, cur_u)
        occ_right = contract('ik,pkj->pij', cur_do, cur_u) + contract('ik,pkj->pij', cur_uo, next_b)
        virt_left = contract('pik,jk->pij', cur_b, prev_uv) + contract('pki,kj->pij', prev_u, prev_dv)
        virt_mid = contract('pki,kj->pij', prev_u, prev_uv) + contract('pik,kj->pij', cur_b, cur_dv) + contract('pik,jk->pij', cur_u, cur_uv)
        virt_right = contract('pik,kj->pij', cur_b, cur_uv) + contract('pik,kj->pij', cur_u, next_dv)
        occ_all = jnp.stack([occ_left, occ_mid, occ_right], axis=1).reshape(AUX, 3 * BS * BS)
        virt_all = jnp.stack([virt_left, virt_mid, virt_right], axis=1).reshape(AUX, 3 * BS * BS)
        running = running + lax.dot_general(occ_all, virt_all, (((1,), (1,)), ((), ())), precision=HIGHEST, preferred_element_type=jnp.float32)
        return (running, None)
    running, unused = lax.scan(row_step, jnp.zeros((AUX, AUX), jnp.float32), jnp.arange(NB, dtype=jnp.int32))
    return running / jnp.sqrt(jnp.float32(3 * NB * BS * BS))
```

```python
import functools
import math

import jax
import jax.numpy as jnp
from jax import lax
from jax.experimental import pallas as pl
from jax.experimental.pallas import tpu as pltpu
from jax.sharding import PartitionSpec as P

BS = 64
NB = 96
NX, NZ = 4, 16
N_ORB = NX * NZ
PAIRS = 8
CP = 2 * PAIRS
CL = CP * BS
NK = 98
HK = NK // 2
MESH = pl.DeviceIdType.MESH
F32, BF16 = jnp.float32, jnp.bfloat16


def split(value):
    high = value.astype(BF16)
    return high, (value - high.astype(F32)).astype(BF16)


def dot3(first, second, dims=(((1,), (0,)), ((), ()))):
    (fh, fl), (sh, sl) = first, second
    dot = functools.partial(lax.dot_general, dimension_numbers=dims, preferred_element_type=F32)
    return dot(fh, sh) + dot(fh, sl) + dot(fl, sh)


def flip(pair):
    turned = pair.T
    return jnp.concatenate([turned[:BS], turned[BS:]], axis=1)


def swap(first, second, left):
    even = jnp.where(left, first, pltpu.roll(second, BS, 1))
    odd = jnp.where(left, pltpu.roll(first, BS, 1), second)
    return even, odd


def twice(block):
    zero = jnp.zeros((BS, BS), F32)
    return jnp.concatenate(
        [jnp.concatenate([block, zero], axis=1), jnp.concatenate([zero, block], axis=1)], axis=0
    )


def kernel(
    scale, tc, go, gv, counts, pattern, out,
    um, lastb, rimp, rimn, gl_s, gl_r, gf_s, gf_r, buf_b, buf_d, got_b, got_d, stage, corner,
    l1, l2, wd, we, chi, rx, zb, rz, fs, rf,
    rim_send, rim_recv, g_send, g_recv, y_send, y_recv, y_local, x_send, x_recv, z_send, z_recv, f_send, f_recv,
):
    chunks = tc.shape[3] // CL
    o, a = lax.axis_index("orb"), lax.axis_index("aux")
    x, z, y, c = o // NZ, o % NZ, a // 2, a % 2
    y1, y3 = y + 1 - 2 * (y % 2), 3 - y
    yd, yb = y1 * (1 - c) + y3 * c, y3 * (1 - c) + y1 * c
    behind, ahead = (o + N_ORB - 1) % N_ORB, (o + 1) % N_ORB

    sources = []
    for cs in range(2):
        kept, other = (y3, y1) if cs == 0 else (y1, y3)
        here = jnp.logical_or(x == y, x == kept)
        ys = jnp.where(here, y, other)
        xs = jnp.where(here, c, 2 + c)
        mine = jnp.logical_and(jnp.logical_and(xs == x, ys == y), c == cs)
        sources.append((xs * NZ + z, ys * 2 + cs, mine))
    yf, cf = jnp.where(x < 2, y, yd), x % 2
    same = jnp.logical_and(yf == y, cf == c)
    targets = [
        (y * NZ + z, yf * 2 + cf, jnp.logical_and(same, x == y)),
        (yb * NZ + z, yf * 2 + cf, jnp.logical_and(same, x == yb)),
    ]

    barrier = pltpu.get_barrier_semaphore()

    def greet(orb, aux):
        pl.semaphore_signal(barrier, inc=1, device_id=(orb, aux), device_id_type=MESH)

    greet(behind, a)
    greet(ahead, a)
    for aux in (y * 2 + 1 - c, y1 * 2, y1 * 2 + 1, y3 * 2, y3 * 2 + 1):
        greet(o, aux)
    for step in range(1, NX):
        greet((x + step) % NX * NZ + z, a)

    @pl.loop(1, NZ)
    def _(step):
        greet(x * NZ + (z + step) % NZ, a)

    for orb, aux, mine in sources:
        pl.when(jnp.logical_not(mine))(functools.partial(greet, orb, aux))

    own = counts[o]
    start = lax.fori_loop(0, N_ORB, lambda i, s: s + jnp.where(i < o, counts[i], 0), jnp.int32(0))
    two = (own > 1).astype(F32)
    one = 1.0 - two
    ok0 = (start < NB - 1).astype(F32)
    ok1 = (start + 1 < NB - 1).astype(F32) * two
    m0 = [pattern[0, i].astype(F32) * ok0 for i in range(3)]
    m1 = [pattern[1, i].astype(F32) * ok1 for i in range(3)]

    uo = [go[0, 1] * m0[1], go[1, 1] * m1[1]]
    uv = [gv[0, 1] * m0[2], gv[1, 1] * m1[2]]
    gl_s[0] = uo[0] * one + uo[1]
    gl_s[1] = uv[0] * one + uv[1]
    gf_s[0] = go[0, 0]
    gf_s[1] = uo[0]
    gf_s[2] = gv[0, 0]

    @pl.loop(0, tc.shape[3] // 512)
    def _(i):
        lanes = pl.ds(pl.multiple_of(i * 512, 512), 512)
        u0, u1 = tc[0, 1, :, lanes] * m0[0], tc[1, 1, :, lanes] * m1[0]
        um[0, :, lanes] = u0
        um[1, :, lanes] = u1
        lastb[0, :, lanes] = tc[0, 0, :, lanes] * one + tc[1, 0, :, lanes] * two
        lastb[1, :, lanes] = u0 * one + u1

    away = [1 - mine.astype(jnp.int32) for _, _, mine in targets]
    pl.semaphore_wait(barrier, 7 + NX - 1 + NZ - 1 + away[0] + away[1])

    def remote(src, dst, send, recv, orb, aux):
        return pltpu.make_async_remote_copy(
            src_ref=src, dst_ref=dst, send_sem=send, recv_sem=recv,
            device_id=(orb, aux), device_id_type=MESH,
        )

    def green_copies():
        return [
            remote(gl_s, gl_r, g_send.at[0], g_recv.at[0], ahead, a),
            remote(gf_s, gf_r, g_send.at[1], g_recv.at[1], behind, a),
        ]

    def rim_copies(ch):
        lanes = pl.ds(pl.multiple_of(ch * CL, CL), CL)
        return [
            remote(lastb.at[:, :, lanes], rimp.at[:, :, lanes], rim_send.at[0, ch], rim_recv.at[0, ch], ahead, a),
            remote(tc.at[0, 0, :, lanes], rimn.at[0, :, lanes], rim_send.at[1, ch], rim_recv.at[1, ch], behind, a),
            remote(um.at[0, :, lanes], rimn.at[1, :, lanes], rim_send.at[2, ch], rim_recv.at[2, ch], behind, a),
        ]

    for copy in green_copies():
        copy.start()

    @pl.loop(0, chunks)
    def _(ch):
        for copy in rim_copies(ch):
            copy.start()

    def y_copies(which, ch):
        buf, got = (buf_b, got_b) if which == 0 else (buf_d, got_d)
        near = [y3, y1] if which == 0 else [y1, y3]
        rows = pl.ds(pl.multiple_of(ch * CP, CP), CP)

        def place(block):
            return pl.ds(pl.multiple_of(block * BS + ch * CP, CP), CP)

        made = [
            remote(
                buf.at[pl.ds((1 - c) * HK, HK), rows], got.at[:, place(c)],
                y_send.at[which, 0, ch], y_recv.at[which, 0, ch], o, y * 2 + 1 - c,
            )
        ]
        for ct in range(2):
            made.append(
                remote(
                    buf.at[pl.ds(ct * HK, HK), rows], got.at[:, place(2 + c)],
                    y_send.at[which, 1 + ct, ch], y_recv.at[which, 1 + c, ch], o, near[ct] * 2 + ct,
                )
            )
        made.append(
            pltpu.make_async_copy(
                buf.at[pl.ds(c * HK, HK), rows], got.at[:, place(c)], y_local.at[which, ch]
            )
        )
        return made

    def y_arrivals(which, ch):
        got = got_b if which == 0 else got_d
        buf = buf_b if which == 0 else buf_d
        rows = pl.ds(pl.multiple_of(ch * CP, CP), CP)
        for j, block in enumerate((1 - c, 2, 3)):
            place = pl.ds(pl.multiple_of(block * BS + ch * CP, CP), CP)
            remote(
                buf.at[pl.ds(0, HK), rows], got.at[:, place],
                y_send.at[which, j, ch], y_recv.at[which, j, ch], o, y * 2 + 1 - c,
            ).wait_recv()

    lane = lax.broadcasted_iota(jnp.int32, (BS // 2, 2 * BS), 1)
    row = lax.broadcasted_iota(jnp.int32, (BS // 2, 2 * BS), 0)
    left = lane < BS
    column = lane % BS
    over, on = column > row, column == row
    far = column == row + BS // 2
    left_row = lax.broadcasted_iota(jnp.int32, (1, 2 * BS), 1) < BS
    half = BS // 2

    def triangle(full, diagonal):
        shifted = pltpu.roll(full[half:], 2 * BS - half, 1)
        packed = jnp.where(over, full[:half], jnp.where(on, diagonal[:half], shifted))
        return packed, jnp.sum(jnp.where(far, diagonal[half:], 0.0), axis=0, keepdims=True)

    def put(buf, ch, edges, fulls, diagonals):
        for p in range(PAIRS):
            even, odd = (slice(2 * p * half, (2 * p + 1) * half), slice((2 * p + 1) * half, (2 * p + 2) * half))
            for s in range(2):
                block = edges[s][p]
                stage[s, even], stage[s, odd] = swap(block[:half], block[half:], left)
            packed, corners = zip(*(triangle(fulls[s][p], diagonals[s][p]) for s in range(2)))
            stage[2, even], stage[2, odd] = swap(packed[0], packed[1], left)
            corner[2 * p : 2 * p + 1], corner[2 * p + 1 : 2 * p + 2] = swap(corners[0], corners[1], left_row)
        rows = pl.ds(pl.multiple_of(ch * CP, CP), CP)
        for kind in range(3):
            for k in range(half):
                buf[kind * half + k, rows] = stage[kind, pl.ds(k, CP, stride=half)]
        buf[3 * half, rows] = corner[...]
        buf[3 * half + 1, rows] = jnp.zeros((CP, 2 * BS), F32)

    def pairs_of(value):
        return [value[:, 2 * BS * p : 2 * BS * (p + 1)] for p in range(PAIRS)]

    @pl.loop(0, chunks)
    def _(ch):
        lanes = pl.ds(pl.multiple_of(ch * CL, CL), CL)
        edges = [pairs_of(um[s, :, lanes]) for s in range(2)]
        diagonals = [pairs_of(tc[0, 0, :, lanes]), pairs_of(tc[1, 0, :, lanes] * two)]
        put(buf_b, ch, edges, diagonals, diagonals)
        for copy in y_copies(0, ch):
            copy.start()

    for copy in green_copies():
        copy.wait()
    do = [None, go[0, 0], go[1, 0] * two + gf_r[0] * one, gf_r[0]]
    uo = [gl_r[0], uo[0], uo[1] + gf_r[1] * one, gf_r[1]]
    dv = [None, gv[0, 0], gv[1, 0] * two + gf_r[2] * one, gf_r[2]]
    uv = [gl_r[1], uv[0], uv[1], None]
    no = jnp.zeros((BS, BS), F32)

    def store(ref, s, value):
        ref[s, 0], ref[s, 1] = split(value)

    def grid(rows):
        return jnp.concatenate([jnp.concatenate(r, axis=1) for r in rows], axis=0)

    for s in range(2):
        n = s + 1
        store(l1, s, grid([
            [uo[n - 1].T, do[n], no, no],
            [uo[n - 1].T, do[n], uo[n], no],
            [uv[n - 1].T, no, no, no],
            [no, dv[n], uv[n], no],
            [no, no, no, uo[n - 1].T],
        ]))
        store(l2, s, grid([
            [do[n], uo[n], no, no],
            [dv[n], uv[n], no, no],
            [dv[n], no, no, no],
            [no, no, uv[n], no],
        ]))
        right = [uv[n - 1], dv[n], uv[n].T, do[n], uo[n].T]
        store(wd, s, jnp.concatenate([twice(r) for r in right], axis=0))
        right = [uv[n], dv[n + 1], uo[n], do[n + 1], uo[n + 1].T]
        store(we, s, jnp.concatenate([twice(r) for r in right], axis=0))

    def stacked(value):
        return jnp.concatenate(pairs_of(value), axis=0)

    @pl.loop(0, chunks)
    def _(ch):
        for copy in rim_copies(ch):
            copy.wait()
        lanes = pl.ds(pl.multiple_of(ch * CL, CL), CL)
        diag = [rimp[0, :, lanes], tc[0, 0, :, lanes],
                tc[1, 0, :, lanes] * two + rimn[0, :, lanes] * one, rimn[0, :, lanes]]
        upper = [rimp[1, :, lanes], um[0, :, lanes],
                 um[1, :, lanes] + rimn[1, :, lanes] * one, rimn[1, :, lanes]]
        edges, fulls, diagonals = [], [], []
        for s in range(2):
            n = s + 1
            turned = jnp.concatenate([flip(b) for b in pairs_of(upper[n])], axis=1)
            s1 = split(jnp.concatenate([upper[n - 1], diag[n], turned, diag[n - 1]], axis=0))
            s2 = split(jnp.concatenate([upper[n], diag[n + 1], upper[n + 1], diag[n]], axis=0))
            t1 = split(dot3((l1[s, 0], l1[s, 1]), s1))
            t2 = split(dot3((l2[s, 0], l2[s, 1]), s2))

            def take(picks):
                return [
                    jnp.concatenate([stacked((t1, t2)[w][part][BS * r : BS * (r + 1)]) for w, r in picks], axis=1)
                    for part in range(2)
                ]

            d = dot3(take([(0, 4), (0, 0), (1, 0), (0, 2), (1, 2)]), (wd[s, 0], wd[s, 1]))
            e = dot3(take([(0, 1), (1, 0), (0, 3), (1, 1), (1, 3)]), (we[s, 0], we[s, 1]))
            d = [d[BS * p : BS * (p + 1)] for p in range(PAIRS)]
            edges.append([e[BS * p : BS * (p + 1)] for p in range(PAIRS)])
            diagonals.append(d)
            fulls.append([b + flip(b) for b in d])
        put(buf_d, ch, edges, fulls, diagonals)
        for copy in y_copies(1, ch):
            copy.start()

    chi[...] = jnp.zeros_like(chi)
    for which in range(2):

        @pl.loop(0, chunks)
        def _(ch):
            y_arrivals(which, ch)
            made = y_copies(which, ch)
            for copy in made[:3]:
                copy.wait_send()
            made[3].wait()

    @pl.loop(0, HK // 7)
    def _(g):
        d = split(jnp.concatenate([got_d[g * 7 + i] for i in range(7)], axis=1))
        b = split(jnp.concatenate([got_b[g * 7 + i] for i in range(7)], axis=1))
        chi[...] += dot3(d, b, (((1,), (1,)), ((), ())))

    def x_copy(step):
        there = (x + step) % NX
        return remote(
            chi.at[pl.ds(pl.multiple_of(there * BS, BS), BS)], rx.at[step - 1],
            x_send.at[step - 1], x_recv.at[step - 1], there * NZ + z, a,
        )

    for step in range(1, NX):
        x_copy(step).start()
    for step in range(1, NX):
        x_copy(step).wait()
    part = chi[pl.ds(pl.multiple_of(x * BS, BS), BS), :] + rx[0] + rx[1] + rx[2]
    turned = part.T
    zb[...] = jnp.concatenate([turned[: 2 * BS], turned[2 * BS :]], axis=1).reshape(NZ, 8, 2 * BS)

    def z_copy(step):
        there = (z + step) % NZ
        return remote(
            zb.at[there], rz.at[step - 1], z_send.at[step - 1], z_recv.at[step - 1], x * NZ + there, a
        )

    @pl.loop(1, NZ)
    def _(step):
        z_copy(step).start()

    @pl.loop(1, NZ)
    def _(step):
        z_copy(step).wait()

    total = zb[z]
    for i in range(NZ - 1):
        total = total + rz[i]
    fs[0] = total
    fs[1] = pltpu.roll(total, BS, 1)

    def f_copy(i):
        orb, aux, _ = targets[i]
        return remote(fs.at[i], rf.at[c], f_send.at[i], f_recv.at[c], orb, aux)

    for i in range(2):
        mine = targets[i][2]

        @pl.when(mine)
        def _():
            rf[c] = fs[i]

        @pl.when(jnp.logical_not(mine))
        def _():
            f_copy(i).start()

    for cs in range(2):

        @pl.when(jnp.logical_not(sources[cs][2]))
        def _():
            remote(fs.at[0], rf.at[cs], f_send.at[0], f_recv.at[cs], o, y * 2 + 1 - c).wait_recv()

    for i in range(2):

        @pl.when(jnp.logical_not(targets[i][2]))
        def _():
            f_copy(i).wait_send()

    out[...] = (rf[0] + rf[1])[:, :BS] * scale


def local(three_centre, green_occ, green_virt, owned_counts, pattern):
    slots, _, _, lanes = three_centre.shape
    chunks = lanes // CL
    aux_local = lanes // BS
    shape = (slots, 2, BS, BS)
    vmem, dma = pltpu.VMEM, pltpu.SemaphoreType.DMA
    smem = pl.BlockSpec(memory_space=pltpu.SMEM)
    block = pl.BlockSpec(memory_space=pltpu.VMEM)
    made = pl.pallas_call(
        functools.partial(kernel, 1.0 / math.sqrt(3 * NB * BS * BS)),
        out_shape=jax.ShapeDtypeStruct((8, BS), F32),
        in_specs=[block, block, block, smem, smem],
        out_specs=block,
        scratch_shapes=[
            vmem((2, BS, lanes), F32),
            vmem((2, BS, lanes), F32),
            vmem((2, BS, lanes), F32),
            vmem((2, BS, lanes), F32),
            vmem((2, BS, BS), F32),
            vmem((2, BS, BS), F32),
            vmem((3, BS, BS), F32),
            vmem((3, BS, BS), F32),
            vmem((NK, aux_local, 2 * BS), F32),
            vmem((NK, aux_local, 2 * BS), F32),
            vmem((HK, 4 * aux_local, 2 * BS), F32),
            vmem((HK, 4 * aux_local, 2 * BS), F32),
            vmem((3, CP * BS // 2, 2 * BS), F32),
            vmem((CP, 2 * BS), F32),
            vmem((2, 2, 5 * BS, 4 * BS), BF16),
            vmem((2, 2, 4 * BS, 4 * BS), BF16),
            vmem((2, 2, 10 * BS, 2 * BS), BF16),
            vmem((2, 2, 10 * BS, 2 * BS), BF16),
            vmem((4 * aux_local, 4 * aux_local), F32),
            vmem((NX - 1, aux_local, 4 * aux_local), F32),
            vmem((NZ, 8, 2 * BS), F32),
            vmem((NZ - 1, 8, 2 * BS), F32),
            vmem((2, 8, 2 * BS), F32),
            vmem((2, 8, 2 * BS), F32),
            dma((3, chunks)),
            dma((3, chunks)),
            dma((2,)),
            dma((2,)),
            dma((2, 3, chunks)),
            dma((2, 3, chunks)),
            dma((2, chunks)),
            dma((NX - 1,)),
            dma((NX - 1,)),
            dma((NZ - 1,)),
            dma((NZ - 1,)),
            dma((2,)),
            dma((2,)),
        ],
        compiler_params=pltpu.CompilerParams(
            collective_id=0, has_side_effects=True, vmem_limit_bytes=56 * 2**20
        ),
    )(
        three_centre,
        green_occ.reshape(shape),
        green_virt.reshape(shape),
        owned_counts,
        pattern,
    )
    return made.T


def solution(mesh):
    placed = (
        P("orb", None, None, "aux"),
        P("orb", None, None),
        P("orb", None, None),
        P(),
        P("orb", None),
    )
    return jax.shard_map(
        local, mesh=mesh, in_specs=placed, out_specs=P("aux", "orb"), check_vma=False
    )
```

```python
import functools
import math

import jax
import jax.numpy as jnp
from jax import lax
from jax.experimental import pallas as pl
from jax.experimental.pallas import tpu as pltpu
from jax.sharding import PartitionSpec as P

BS = 64
NB = 96
NX, NZ = 4, 16
N_ORB = NX * NZ
PAIRS = 8
CP = 2 * PAIRS
CL = CP * BS
NK = 98
HK = NK // 2
MESH = pl.DeviceIdType.MESH
F32, BF16 = jnp.float32, jnp.bfloat16


def split(value):
    high = value.astype(BF16)
    return high, (value - high.astype(F32)).astype(BF16)


def dot3(first, second, dims=(((1,), (0,)), ((), ()))):
    (fh, fl), (sh, sl) = first, second
    dot = functools.partial(lax.dot_general, dimension_numbers=dims, preferred_element_type=F32)
    return dot(fh, sh) + dot(fh, sl) + dot(fl, sh)


def flip(pair):
    turned = pair.T
    return jnp.concatenate([turned[:BS], turned[BS:]], axis=1)


def swap(first, second, left):
    even = jnp.where(left, first, pltpu.roll(second, BS, 1))
    odd = jnp.where(left, pltpu.roll(first, BS, 1), second)
    return even, odd


def twice(block):
    zero = jnp.zeros((BS, BS), F32)
    return jnp.concatenate(
        [jnp.concatenate([block, zero], axis=1), jnp.concatenate([zero, block], axis=1)], axis=0
    )


def kernel(
    scale, tc, go_rows, gv_rows, counts, pattern, out,
    go, gv, fold, um, lastb, rimp, rimn, gl_s, gl_r, gf_s, gf_r, buf_b, buf_d, got_b, got_d, stage, corner,
    l1, l2, wd, we, chi, rx, zb, rz, fs, rf,
    rim_send, rim_recv, g_send, g_recv, y_send, y_recv, y_local, x_send, x_recv, z_send, z_recv, f_send, f_recv,
):
    chunks = tc.shape[3] // CL
    o, a = lax.axis_index("orb"), lax.axis_index("aux")
    x, z, y, c = o // NZ, o % NZ, a // 2, a % 2
    y1, y3 = y + 1 - 2 * (y % 2), 3 - y
    yd, yb = y1 * (1 - c) + y3 * c, y3 * (1 - c) + y1 * c
    behind, ahead = (o + N_ORB - 1) % N_ORB, (o + 1) % N_ORB

    sources = []
    for cs in range(2):
        kept, other = (y3, y1) if cs == 0 else (y1, y3)
        here = jnp.logical_or(x == y, x == kept)
        ys = jnp.where(here, y, other)
        xs = jnp.where(here, c, 2 + c)
        mine = jnp.logical_and(jnp.logical_and(xs == x, ys == y), c == cs)
        sources.append((xs * NZ + z, ys * 2 + cs, mine))
    yf, cf = jnp.where(x < 2, y, yd), x % 2
    same = jnp.logical_and(yf == y, cf == c)
    targets = [
        (y * NZ + z, yf * 2 + cf, jnp.logical_and(same, x == y)),
        (yb * NZ + z, yf * 2 + cf, jnp.logical_and(same, x == yb)),
    ]

    barrier = pltpu.get_barrier_semaphore()

    def greet(orb, aux):
        pl.semaphore_signal(barrier, inc=1, device_id=(orb, aux), device_id_type=MESH)

    greet(behind, a)
    greet(ahead, a)
    for aux in (y * 2 + 1 - c, y1 * 2, y1 * 2 + 1, y3 * 2, y3 * 2 + 1):
        greet(o, aux)
    for step in range(1, NX):
        greet((x + step) % NX * NZ + z, a)

    @pl.loop(1, NZ)
    def _(step):
        greet(x * NZ + (z + step) % NZ, a)

    for orb, aux, mine in sources:
        pl.when(jnp.logical_not(mine))(functools.partial(greet, orb, aux))

    own = counts[o]
    start = lax.fori_loop(0, N_ORB, lambda i, s: s + jnp.where(i < o, counts[i], 0), jnp.int32(0))
    two = (own > 1).astype(F32)
    one = 1.0 - two
    ok0 = (start < NB - 1).astype(F32)
    ok1 = (start + 1 < NB - 1).astype(F32) * two
    m0 = [pattern[0, i].astype(F32) * ok0 for i in range(3)]
    m1 = [pattern[1, i].astype(F32) * ok1 for i in range(3)]

    for rows, wide in ((go_rows, go), (gv_rows, gv)):
        for s in range(2):
            for kind in range(2):
                for r in range(BS // 2):
                    fold[r : r + 1] = rows[s, kind : kind + 1, 2 * BS * r : 2 * BS * (r + 1)]
                folded = fold[...]
                wide[s, kind, pl.ds(0, BS // 2, stride=2)] = folded
                wide[s, kind, pl.ds(1, BS // 2, stride=2)] = pltpu.roll(folded, BS, 1)

    def green(blocks, s, kind):
        return blocks[s, kind][:, :BS]

    uo = [green(go, 0, 1) * m0[1], green(go, 1, 1) * m1[1]]
    uv = [green(gv, 0, 1) * m0[2], green(gv, 1, 1) * m1[2]]
    gl_s[0] = uo[0] * one + uo[1]
    gl_s[1] = uv[0] * one + uv[1]
    gf_s[0] = green(go, 0, 0)
    gf_s[1] = uo[0]
    gf_s[2] = green(gv, 0, 0)

    @pl.loop(0, tc.shape[3] // 512)
    def _(i):
        lanes = pl.ds(pl.multiple_of(i * 512, 512), 512)
        u0, u1 = tc[0, 1, :, lanes] * m0[0], tc[1, 1, :, lanes] * m1[0]
        um[0, :, lanes] = u0
        um[1, :, lanes] = u1
        lastb[0, :, lanes] = tc[0, 0, :, lanes] * one + tc[1, 0, :, lanes] * two
        lastb[1, :, lanes] = u0 * one + u1

    def remote(src, dst, send, recv, orb, aux):
        return pltpu.make_async_remote_copy(
            src_ref=src, dst_ref=dst, send_sem=send, recv_sem=recv,
            device_id=(orb, aux), device_id_type=MESH,
        )

    def green_copies():
        return [
            remote(gl_s, gl_r, g_send.at[0], g_recv.at[0], ahead, a),
            remote(gf_s, gf_r, g_send.at[1], g_recv.at[1], behind, a),
        ]

    def rim_copies(ch):
        lanes = pl.ds(pl.multiple_of(ch * CL, CL), CL)
        return [
            remote(lastb.at[:, :, lanes], rimp.at[:, :, lanes], rim_send.at[0, ch], rim_recv.at[0, ch], ahead, a),
            remote(tc.at[0, 0, :, lanes], rimn.at[0, :, lanes], rim_send.at[1, ch], rim_recv.at[1, ch], behind, a),
            remote(um.at[0, :, lanes], rimn.at[1, :, lanes], rim_send.at[2, ch], rim_recv.at[2, ch], behind, a),
        ]

    def y_copies(which, ch):
        buf, got = (buf_b, got_b) if which == 0 else (buf_d, got_d)
        near = [y3, y1] if which == 0 else [y1, y3]
        rows = pl.ds(pl.multiple_of(ch * CP, CP), CP)

        def place(block):
            return pl.ds(pl.multiple_of(block * BS + ch * CP, CP), CP)

        made = [
            remote(
                buf.at[pl.ds((1 - c) * HK, HK), rows], got.at[:, place(c)],
                y_send.at[which, 0, ch], y_recv.at[which, 0, ch], o, y * 2 + 1 - c,
            )
        ]
        for ct in range(2):
            made.append(
                remote(
                    buf.at[pl.ds(ct * HK, HK), rows], got.at[:, place(2 + c)],
                    y_send.at[which, 1 + ct, ch], y_recv.at[which, 1 + c, ch], o, near[ct] * 2 + ct,
                )
            )
        made.append(
            pltpu.make_async_copy(
                buf.at[pl.ds(c * HK, HK), rows], got.at[:, place(c)], y_local.at[which, ch]
            )
        )
        return made

    def y_arrivals(which, ch):
        got = got_b if which == 0 else got_d
        buf = buf_b if which == 0 else buf_d
        rows = pl.ds(pl.multiple_of(ch * CP, CP), CP)
        for j, block in enumerate((1 - c, 2, 3)):
            place = pl.ds(pl.multiple_of(block * BS + ch * CP, CP), CP)
            remote(
                buf.at[pl.ds(0, HK), rows], got.at[:, place],
                y_send.at[which, j, ch], y_recv.at[which, j, ch], o, y * 2 + 1 - c,
            ).wait_recv()

    lane = lax.broadcasted_iota(jnp.int32, (BS // 2, 2 * BS), 1)
    row = lax.broadcasted_iota(jnp.int32, (BS // 2, 2 * BS), 0)
    left = lane < BS
    column = lane % BS
    over, on = column > row, column == row
    far = column == row + BS // 2
    left_row = lax.broadcasted_iota(jnp.int32, (1, 2 * BS), 1) < BS
    half = BS // 2

    def triangle(full, diagonal):
        shifted = pltpu.roll(full[half:], 2 * BS - half, 1)
        packed = jnp.where(over, full[:half], jnp.where(on, diagonal[:half], shifted))
        return packed, jnp.sum(jnp.where(far, diagonal[half:], 0.0), axis=0, keepdims=True)

    def put(buf, ch, edges, fulls, diagonals):
        for p in range(PAIRS):
            even, odd = (slice(2 * p * half, (2 * p + 1) * half), slice((2 * p + 1) * half, (2 * p + 2) * half))
            for s in range(2):
                block = edges[s][p]
                stage[s, even], stage[s, odd] = swap(block[:half], block[half:], left)
            packed, corners = zip(*(triangle(fulls[s][p], diagonals[s][p]) for s in range(2)))
            stage[2, even], stage[2, odd] = swap(packed[0], packed[1], left)
            corner[2 * p : 2 * p + 1], corner[2 * p + 1 : 2 * p + 2] = swap(corners[0], corners[1], left_row)
        rows = pl.ds(pl.multiple_of(ch * CP, CP), CP)
        for kind in range(3):
            for k in range(half):
                buf[kind * half + k, rows] = stage[kind, pl.ds(k, CP, stride=half)]
        buf[3 * half, rows] = corner[...]
        buf[3 * half + 1, rows] = jnp.zeros((CP, 2 * BS), F32)

    def pairs_of(value):
        return [value[:, 2 * BS * p : 2 * BS * (p + 1)] for p in range(PAIRS)]

    def pack_b(ch):
        lanes = pl.ds(pl.multiple_of(ch * CL, CL), CL)
        edges = [pairs_of(um[s, :, lanes]) for s in range(2)]
        diagonals = [pairs_of(tc[0, 0, :, lanes]), pairs_of(tc[1, 0, :, lanes] * two)]
        put(buf_b, ch, edges, diagonals, diagonals)

    pack_b(0)
    away = [1 - mine.astype(jnp.int32) for _, _, mine in targets]
    pl.semaphore_wait(barrier, 7 + NX - 1 + NZ - 1 + away[0] + away[1])

    for copy in y_copies(0, 0):
        copy.start()

    for copy in green_copies():
        copy.start()

    @pl.loop(0, chunks)
    def _(ch):
        for copy in rim_copies(ch):
            copy.start()

    @pl.loop(1, chunks)
    def _(ch):
        pack_b(ch)
        for copy in y_copies(0, ch):
            copy.start()

    for copy in green_copies():
        copy.wait()
    do = [None, green(go, 0, 0), green(go, 1, 0) * two + gf_r[0] * one, gf_r[0]]
    uo = [gl_r[0], uo[0], uo[1] + gf_r[1] * one, gf_r[1]]
    dv = [None, green(gv, 0, 0), green(gv, 1, 0) * two + gf_r[2] * one, gf_r[2]]
    uv = [gl_r[1], uv[0], uv[1], None]
    no = jnp.zeros((BS, BS), F32)

    def store(ref, s, value):
        ref[s, 0], ref[s, 1] = split(value)

    def grid(rows):
        return jnp.concatenate([jnp.concatenate(r, axis=1) for r in rows], axis=0)

    for s in range(2):
        n = s + 1
        store(l1, s, grid([
            [uo[n - 1].T, do[n], no, no],
            [uo[n - 1].T, do[n], uo[n], no],
            [uv[n - 1].T, no, no, no],
            [no, dv[n], uv[n], no],
            [no, no, no, uo[n - 1].T],
        ]))
        store(l2, s, grid([
            [do[n], uo[n], no, no],
            [dv[n], uv[n], no, no],
            [dv[n], no, no, no],
            [no, no, uv[n], no],
        ]))
        right = [uv[n - 1], dv[n], uv[n].T, do[n], uo[n].T]
        store(wd, s, jnp.concatenate([twice(r) for r in right], axis=0))
        right = [uv[n], dv[n + 1], uo[n], do[n + 1], uo[n + 1].T]
        store(we, s, jnp.concatenate([twice(r) for r in right], axis=0))

    def stacked(value):
        return jnp.concatenate(pairs_of(value), axis=0)

    @pl.loop(0, chunks)
    def _(ch):
        for copy in rim_copies(ch):
            copy.wait()
        lanes = pl.ds(pl.multiple_of(ch * CL, CL), CL)
        diag = [rimp[0, :, lanes], tc[0, 0, :, lanes],
                tc[1, 0, :, lanes] * two + rimn[0, :, lanes] * one, rimn[0, :, lanes]]
        upper = [rimp[1, :, lanes], um[0, :, lanes],
                 um[1, :, lanes] + rimn[1, :, lanes] * one, rimn[1, :, lanes]]
        edges, fulls, diagonals = [], [], []
        for s in range(2):
            n = s + 1
            turned = jnp.concatenate([flip(b) for b in pairs_of(upper[n])], axis=1)
            s1 = split(jnp.concatenate([upper[n - 1], diag[n], turned, diag[n - 1]], axis=0))
            s2 = split(jnp.concatenate([upper[n], diag[n + 1], upper[n + 1], diag[n]], axis=0))
            t1 = split(dot3((l1[s, 0], l1[s, 1]), s1))
            t2 = split(dot3((l2[s, 0], l2[s, 1]), s2))

            def take(picks):
                return [
                    jnp.concatenate([stacked((t1, t2)[w][part][BS * r : BS * (r + 1)]) for w, r in picks], axis=1)
                    for part in range(2)
                ]

            d = dot3(take([(0, 4), (0, 0), (1, 0), (0, 2), (1, 2)]), (wd[s, 0], wd[s, 1]))
            e = dot3(take([(0, 1), (1, 0), (0, 3), (1, 1), (1, 3)]), (we[s, 0], we[s, 1]))
            d = [d[BS * p : BS * (p + 1)] for p in range(PAIRS)]
            edges.append([e[BS * p : BS * (p + 1)] for p in range(PAIRS)])
            diagonals.append(d)
            fulls.append([b + flip(b) for b in d])
        put(buf_d, ch, edges, fulls, diagonals)
        for copy in y_copies(1, ch):
            copy.start()

    chi[...] = jnp.zeros_like(chi)
    for which in range(2):

        @pl.loop(0, chunks)
        def _(ch):
            y_arrivals(which, ch)
            made = y_copies(which, ch)
            for copy in made[:3]:
                copy.wait_send()
            made[3].wait()

    @pl.loop(0, HK // 7)
    def _(g):
        d = split(jnp.concatenate([got_d[g * 7 + i] for i in range(7)], axis=1))
        b = split(jnp.concatenate([got_b[g * 7 + i] for i in range(7)], axis=1))
        chi[...] += dot3(d, b, (((1,), (1,)), ((), ())))

    def x_copy(step):
        there = (x + step) % NX
        return remote(
            chi.at[pl.ds(pl.multiple_of(there * BS, BS), BS)], rx.at[step - 1],
            x_send.at[step - 1], x_recv.at[step - 1], there * NZ + z, a,
        )

    for step in range(1, NX):
        x_copy(step).start()
    for step in range(1, NX):
        x_copy(step).wait()
    part = chi[pl.ds(pl.multiple_of(x * BS, BS), BS), :] + rx[0] + rx[1] + rx[2]
    turned = part.T
    zb[...] = jnp.concatenate([turned[: 2 * BS], turned[2 * BS :]], axis=1).reshape(NZ, 8, 2 * BS)

    def z_copy(step):
        there = (z + step) % NZ
        return remote(
            zb.at[there], rz.at[step - 1], z_send.at[step - 1], z_recv.at[step - 1], x * NZ + there, a
        )

    @pl.loop(1, NZ)
    def _(step):
        z_copy(step).start()

    @pl.loop(1, NZ)
    def _(step):
        z_copy(step).wait()

    total = zb[z]
    for i in range(NZ - 1):
        total = total + rz[i]
    fs[0] = total
    fs[1] = pltpu.roll(total, BS, 1)

    def f_copy(i):
        orb, aux, _ = targets[i]
        return remote(fs.at[i], rf.at[c], f_send.at[i], f_recv.at[c], orb, aux)

    for i in range(2):
        mine = targets[i][2]

        @pl.when(mine)
        def _():
            rf[c] = fs[i]

        @pl.when(jnp.logical_not(mine))
        def _():
            f_copy(i).start()

    for cs in range(2):

        @pl.when(jnp.logical_not(sources[cs][2]))
        def _():
            remote(fs.at[0], rf.at[cs], f_send.at[0], f_recv.at[cs], o, y * 2 + 1 - c).wait_recv()

    for i in range(2):

        @pl.when(jnp.logical_not(targets[i][2]))
        def _():
            f_copy(i).wait_send()

    out[...] = (rf[0] + rf[1])[:, :BS] * scale


def local(three_centre, green_occ, green_virt, owned_counts, pattern):
    lanes = three_centre.shape[3]
    chunks = lanes // CL
    aux_local = lanes // BS
    vmem, dma = pltpu.VMEM, pltpu.SemaphoreType.DMA
    smem = pl.BlockSpec(memory_space=pltpu.SMEM)
    block = pl.BlockSpec(memory_space=pltpu.VMEM)
    made = pl.pallas_call(
        functools.partial(kernel, 1.0 / math.sqrt(3 * NB * BS * BS)),
        out_shape=jax.ShapeDtypeStruct((8, BS), F32),
        in_specs=[block, block, block, smem, smem],
        out_specs=block,
        scratch_shapes=[
            vmem((2, 2, BS, 2 * BS), F32),
            vmem((2, 2, BS, 2 * BS), F32),
            vmem((BS // 2, 2 * BS), F32),
            vmem((2, BS, lanes), F32),
            vmem((2, BS, lanes), F32),
            vmem((2, BS, lanes), F32),
            vmem((2, BS, lanes), F32),
            vmem((2, BS, BS), F32),
            vmem((2, BS, BS), F32),
            vmem((3, BS, BS), F32),
            vmem((3, BS, BS), F32),
            vmem((NK, aux_local, 2 * BS), F32),
            vmem((NK, aux_local, 2 * BS), F32),
            vmem((HK, 4 * aux_local, 2 * BS), F32),
            vmem((HK, 4 * aux_local, 2 * BS), F32),
            vmem((3, CP * BS // 2, 2 * BS), F32),
            vmem((CP, 2 * BS), F32),
            vmem((2, 2, 5 * BS, 4 * BS), BF16),
            vmem((2, 2, 4 * BS, 4 * BS), BF16),
            vmem((2, 2, 10 * BS, 2 * BS), BF16),
            vmem((2, 2, 10 * BS, 2 * BS), BF16),
            vmem((4 * aux_local, 4 * aux_local), F32),
            vmem((NX - 1, aux_local, 4 * aux_local), F32),
            vmem((NZ, 8, 2 * BS), F32),
            vmem((NZ - 1, 8, 2 * BS), F32),
            vmem((2, 8, 2 * BS), F32),
            vmem((2, 8, 2 * BS), F32),
            dma((3, chunks)),
            dma((3, chunks)),
            dma((2,)),
            dma((2,)),
            dma((2, 3, chunks)),
            dma((2, 3, chunks)),
            dma((2, chunks)),
            dma((NX - 1,)),
            dma((NX - 1,)),
            dma((NZ - 1,)),
            dma((NZ - 1,)),
            dma((2,)),
            dma((2,)),
        ],
        compiler_params=pltpu.CompilerParams(
            collective_id=0, has_side_effects=True, vmem_limit_bytes=56 * 2**20
        ),
    )(
        three_centre,
        green_occ,
        green_virt,
        owned_counts,
        pattern,
    )
    return made.T


def solution(mesh):
    placed = (
        P("orb", None, None, "aux"),
        P("orb", None, None),
        P("orb", None, None),
        P(),
        P("orb", None),
    )
    return jax.shard_map(
        local, mesh=mesh, in_specs=placed, out_specs=P("aux", "orb"), check_vma=False
    )
```

```python
import functools
import math

import jax
import jax.numpy as jnp
from jax import lax
from jax.experimental import pallas as pl
from jax.experimental.pallas import tpu as pltpu
from jax.sharding import PartitionSpec as P

BS = 64
NB = 96
NX, NZ = 4, 16
N_ORB = NX * NZ
PAIRS = 8
CP = 2 * PAIRS
CL = CP * BS
NK = 98
HK = NK // 2
MESH = pl.DeviceIdType.MESH
F32, BF16 = jnp.float32, jnp.bfloat16


def split(value):
    high = value.astype(BF16)
    return high, (value - high.astype(F32)).astype(BF16)


def dot3(first, second, dims=(((1,), (0,)), ((), ()))):
    (fh, fl), (sh, sl) = first, second
    dot = functools.partial(lax.dot_general, dimension_numbers=dims, preferred_element_type=F32)
    return dot(fh, sh) + dot(fh, sl) + dot(fl, sh)


def flip(pair):
    turned = pair.T
    return jnp.concatenate([turned[:BS], turned[BS:]], axis=1)


def swap(first, second, left):
    even = jnp.where(left, first, pltpu.roll(second, BS, 1))
    odd = jnp.where(left, pltpu.roll(first, BS, 1), second)
    return even, odd


def twice(block):
    zero = jnp.zeros((BS, BS), F32)
    return jnp.concatenate(
        [jnp.concatenate([block, zero], axis=1), jnp.concatenate([zero, block], axis=1)], axis=0
    )


def kernel(
    scale, tc, go_rows, gv_rows, counts, pattern, out,
    go, gv, fold, um, lastb, rimp, rimn, gl_s, gl_r, gf_s, gf_r, buf_b, buf_d, got_b, got_d, stage, corner, high_b, low_b,
    l1, l2, wd, we, chi, rx, zb, rz, fs, rf,
    rim_send, rim_recv, g_send, g_recv, y_send, y_recv, y_local, x_send, x_recv, z_send, z_recv, f_send, f_recv,
):
    chunks = tc.shape[3] // CL
    o, a = lax.axis_index("orb"), lax.axis_index("aux")
    x, z, y, c = o // NZ, o % NZ, a // 2, a % 2
    y1, y3 = y + 1 - 2 * (y % 2), 3 - y
    yd, yb = y1 * (1 - c) + y3 * c, y3 * (1 - c) + y1 * c
    behind, ahead = (o + N_ORB - 1) % N_ORB, (o + 1) % N_ORB

    sources = []
    for cs in range(2):
        kept, other = (y3, y1) if cs == 0 else (y1, y3)
        here = jnp.logical_or(x == y, x == kept)
        ys = jnp.where(here, y, other)
        xs = jnp.where(here, c, 2 + c)
        mine = jnp.logical_and(jnp.logical_and(xs == x, ys == y), c == cs)
        sources.append((xs * NZ + z, ys * 2 + cs, mine))
    yf, cf = jnp.where(x < 2, y, yd), x % 2
    same = jnp.logical_and(yf == y, cf == c)
    targets = [
        (y * NZ + z, yf * 2 + cf, jnp.logical_and(same, x == y)),
        (yb * NZ + z, yf * 2 + cf, jnp.logical_and(same, x == yb)),
    ]

    barrier = pltpu.get_barrier_semaphore()

    def greet(orb, aux):
        pl.semaphore_signal(barrier, inc=1, device_id=(orb, aux), device_id_type=MESH)

    greet(behind, a)
    greet(ahead, a)
    for aux in (y * 2 + 1 - c, y1 * 2, y1 * 2 + 1, y3 * 2, y3 * 2 + 1):
        greet(o, aux)
    for step in range(1, NX):
        greet((x + step) % NX * NZ + z, a)

    @pl.loop(1, NZ)
    def _(step):
        greet(x * NZ + (z + step) % NZ, a)

    for orb, aux, mine in sources:
        pl.when(jnp.logical_not(mine))(functools.partial(greet, orb, aux))

    own = counts[o]
    start = lax.fori_loop(0, N_ORB, lambda i, s: s + jnp.where(i < o, counts[i], 0), jnp.int32(0))
    two = (own > 1).astype(F32)
    one = 1.0 - two
    ok0 = (start < NB - 1).astype(F32)
    ok1 = (start + 1 < NB - 1).astype(F32) * two
    m0 = [pattern[0, i].astype(F32) * ok0 for i in range(3)]
    m1 = [pattern[1, i].astype(F32) * ok1 for i in range(3)]

    for rows, wide in ((go_rows, go), (gv_rows, gv)):
        for s in range(2):
            for kind in range(2):
                for r in range(BS // 2):
                    fold[r : r + 1] = rows[s, kind : kind + 1, 2 * BS * r : 2 * BS * (r + 1)]
                folded = fold[...]
                wide[s, kind, pl.ds(0, BS // 2, stride=2)] = folded
                wide[s, kind, pl.ds(1, BS // 2, stride=2)] = pltpu.roll(folded, BS, 1)

    def green(blocks, s, kind):
        return blocks[s, kind][:, :BS]

    uo = [green(go, 0, 1) * m0[1], green(go, 1, 1) * m1[1]]
    uv = [green(gv, 0, 1) * m0[2], green(gv, 1, 1) * m1[2]]
    gl_s[0] = uo[0] * one + uo[1]
    gl_s[1] = uv[0] * one + uv[1]
    gf_s[0] = green(go, 0, 0)
    gf_s[1] = uo[0]
    gf_s[2] = green(gv, 0, 0)

    @pl.loop(0, tc.shape[3] // 512)
    def _(i):
        lanes = pl.ds(pl.multiple_of(i * 512, 512), 512)
        u0, u1 = tc[0, 1, :, lanes] * m0[0], tc[1, 1, :, lanes] * m1[0]
        um[0, :, lanes] = u0
        um[1, :, lanes] = u1
        lastb[0, :, lanes] = tc[0, 0, :, lanes] * one + tc[1, 0, :, lanes] * two
        lastb[1, :, lanes] = u0 * one + u1

    def remote(src, dst, send, recv, orb, aux):
        return pltpu.make_async_remote_copy(
            src_ref=src, dst_ref=dst, send_sem=send, recv_sem=recv,
            device_id=(orb, aux), device_id_type=MESH,
        )

    def green_copies():
        return [
            remote(gl_s, gl_r, g_send.at[0], g_recv.at[0], ahead, a),
            remote(gf_s, gf_r, g_send.at[1], g_recv.at[1], behind, a),
        ]

    def rim_copies(ch):
        lanes = pl.ds(pl.multiple_of(ch * CL, CL), CL)
        return [
            remote(lastb.at[:, :, lanes], rimp.at[:, :, lanes], rim_send.at[0, ch], rim_recv.at[0, ch], ahead, a),
            remote(tc.at[0, 0, :, lanes], rimn.at[0, :, lanes], rim_send.at[1, ch], rim_recv.at[1, ch], behind, a),
            remote(um.at[0, :, lanes], rimn.at[1, :, lanes], rim_send.at[2, ch], rim_recv.at[2, ch], behind, a),
        ]

    def y_copies(which, ch):
        buf, got = (buf_b, got_b) if which == 0 else (buf_d, got_d)
        near = [y3, y1] if which == 0 else [y1, y3]
        rows = pl.ds(pl.multiple_of(ch * CP, CP), CP)

        def place(block):
            return pl.ds(pl.multiple_of(block * BS + ch * CP, CP), CP)

        made = [
            remote(
                buf.at[pl.ds((1 - c) * HK, HK), rows], got.at[:, place(c)],
                y_send.at[which, 0, ch], y_recv.at[which, 0, ch], o, y * 2 + 1 - c,
            )
        ]
        for ct in range(2):
            made.append(
                remote(
                    buf.at[pl.ds(ct * HK, HK), rows], got.at[:, place(2 + c)],
                    y_send.at[which, 1 + ct, ch], y_recv.at[which, 1 + c, ch], o, near[ct] * 2 + ct,
                )
            )
        made.append(
            pltpu.make_async_copy(
                buf.at[pl.ds(c * HK, HK), rows], got.at[:, place(c)], y_local.at[which, ch]
            )
        )
        return made

    def y_arrivals(which, ch):
        got = got_b if which == 0 else got_d
        buf = buf_b if which == 0 else buf_d
        rows = pl.ds(pl.multiple_of(ch * CP, CP), CP)
        for j, block in enumerate((1 - c, 2, 3)):
            place = pl.ds(pl.multiple_of(block * BS + ch * CP, CP), CP)
            remote(
                buf.at[pl.ds(0, HK), rows], got.at[:, place],
                y_send.at[which, j, ch], y_recv.at[which, j, ch], o, y * 2 + 1 - c,
            ).wait_recv()

    lane = lax.broadcasted_iota(jnp.int32, (BS // 2, 2 * BS), 1)
    row = lax.broadcasted_iota(jnp.int32, (BS // 2, 2 * BS), 0)
    left = lane < BS
    column = lane % BS
    over, on = column > row, column == row
    far = column == row + BS // 2
    left_row = lax.broadcasted_iota(jnp.int32, (1, 2 * BS), 1) < BS
    half = BS // 2

    def triangle(full, diagonal):
        shifted = pltpu.roll(full[half:], 2 * BS - half, 1)
        packed = jnp.where(over, full[:half], jnp.where(on, diagonal[:half], shifted))
        return packed, jnp.sum(jnp.where(far, diagonal[half:], 0.0), axis=0, keepdims=True)

    def put(buf, ch, edges, fulls, diagonals):
        for p in range(PAIRS):
            even, odd = (slice(2 * p * half, (2 * p + 1) * half), slice((2 * p + 1) * half, (2 * p + 2) * half))
            for s in range(2):
                block = edges[s][p]
                stage[s, even], stage[s, odd] = swap(block[:half], block[half:], left)
            packed, corners = zip(*(triangle(fulls[s][p], diagonals[s][p]) for s in range(2)))
            stage[2, even], stage[2, odd] = swap(packed[0], packed[1], left)
            corner[2 * p : 2 * p + 1], corner[2 * p + 1 : 2 * p + 2] = swap(corners[0], corners[1], left_row)
        rows = pl.ds(pl.multiple_of(ch * CP, CP), CP)
        for kind in range(3):
            for k in range(half):
                buf[kind * half + k, rows] = stage[kind, pl.ds(k, CP, stride=half)]
        buf[3 * half, rows] = corner[...]
        buf[3 * half + 1, rows] = jnp.zeros((CP, 2 * BS), F32)

    def pairs_of(value):
        return [value[:, 2 * BS * p : 2 * BS * (p + 1)] for p in range(PAIRS)]

    def pack_b(ch):
        lanes = pl.ds(pl.multiple_of(ch * CL, CL), CL)
        edges = [pairs_of(um[s, :, lanes]) for s in range(2)]
        diagonals = [pairs_of(tc[0, 0, :, lanes]), pairs_of(tc[1, 0, :, lanes] * two)]
        put(buf_b, ch, edges, diagonals, diagonals)

    pack_b(0)
    away = [1 - mine.astype(jnp.int32) for _, _, mine in targets]
    pl.semaphore_wait(barrier, 7 + NX - 1 + NZ - 1 + away[0] + away[1])

    for copy in y_copies(0, 0):
        copy.start()

    for copy in green_copies():
        copy.start()

    @pl.loop(0, chunks)
    def _(ch):
        for copy in rim_copies(ch):
            copy.start()

    @pl.loop(1, chunks)
    def _(ch):
        pack_b(ch)
        for copy in y_copies(0, ch):
            copy.start()

    for copy in green_copies():
        copy.wait()
    do = [None, green(go, 0, 0), green(go, 1, 0) * two + gf_r[0] * one, gf_r[0]]
    uo = [gl_r[0], uo[0], uo[1] + gf_r[1] * one, gf_r[1]]
    dv = [None, green(gv, 0, 0), green(gv, 1, 0) * two + gf_r[2] * one, gf_r[2]]
    uv = [gl_r[1], uv[0], uv[1], None]
    no = jnp.zeros((BS, BS), F32)

    def store(ref, s, value):
        ref[s, 0], ref[s, 1] = split(value)

    def grid(rows):
        return jnp.concatenate([jnp.concatenate(r, axis=1) for r in rows], axis=0)

    for s in range(2):
        n = s + 1
        store(l1, s, grid([
            [uo[n - 1].T, do[n], no, no],
            [uo[n - 1].T, do[n], uo[n], no],
            [uv[n - 1].T, no, no, no],
            [no, dv[n], uv[n], no],
            [no, no, no, uo[n - 1].T],
        ]))
        store(l2, s, grid([
            [do[n], uo[n], no, no],
            [dv[n], uv[n], no, no],
            [dv[n], no, no, no],
            [no, no, uv[n], no],
        ]))
        right = [uv[n - 1], dv[n], uv[n].T, do[n], uo[n].T]
        store(wd, s, jnp.concatenate([twice(r) for r in right], axis=0))
        right = [uv[n], dv[n + 1], uo[n], do[n + 1], uo[n + 1].T]
        store(we, s, jnp.concatenate([twice(r) for r in right], axis=0))

    def stacked(value):
        return jnp.concatenate(pairs_of(value), axis=0)

    @pl.loop(0, chunks)
    def _(ch):
        for copy in rim_copies(ch):
            copy.wait()
        lanes = pl.ds(pl.multiple_of(ch * CL, CL), CL)
        diag = [rimp[0, :, lanes], tc[0, 0, :, lanes],
                tc[1, 0, :, lanes] * two + rimn[0, :, lanes] * one, rimn[0, :, lanes]]
        upper = [rimp[1, :, lanes], um[0, :, lanes],
                 um[1, :, lanes] + rimn[1, :, lanes] * one, rimn[1, :, lanes]]
        edges, fulls, diagonals = [], [], []
        for s in range(2):
            n = s + 1
            turned = jnp.concatenate([flip(b) for b in pairs_of(upper[n])], axis=1)
            s1 = split(jnp.concatenate([upper[n - 1], diag[n], turned, diag[n - 1]], axis=0))
            s2 = split(jnp.concatenate([upper[n], diag[n + 1], upper[n + 1], diag[n]], axis=0))
            t1 = split(dot3((l1[s, 0], l1[s, 1]), s1))
            t2 = split(dot3((l2[s, 0], l2[s, 1]), s2))

            def take(picks):
                return [
                    jnp.concatenate([stacked((t1, t2)[w][part][BS * r : BS * (r + 1)]) for w, r in picks], axis=1)
                    for part in range(2)
                ]

            d = dot3(take([(0, 4), (0, 0), (1, 0), (0, 2), (1, 2)]), (wd[s, 0], wd[s, 1]))
            e = dot3(take([(0, 1), (1, 0), (0, 3), (1, 1), (1, 3)]), (we[s, 0], we[s, 1]))
            d = [d[BS * p : BS * (p + 1)] for p in range(PAIRS)]
            edges.append([e[BS * p : BS * (p + 1)] for p in range(PAIRS)])
            diagonals.append(d)
            fulls.append([b + flip(b) for b in d])
        put(buf_d, ch, edges, fulls, diagonals)
        for copy in y_copies(1, ch):
            copy.start()

    chi[...] = jnp.zeros_like(chi)
    for which in range(2):

        @pl.loop(0, chunks)
        def _(ch):
            y_arrivals(which, ch)
            made = y_copies(which, ch)
            for copy in made[:3]:
                copy.wait_send()
            made[3].wait()

        if which == 0:

            @pl.loop(0, HK)
            def _(k):
                high_b[k], low_b[k] = split(got_b[k])

    @pl.loop(0, HK // 7)
    def _(g):
        d = split(jnp.concatenate([got_d[g * 7 + i] for i in range(7)], axis=1))
        b = [jnp.concatenate([ref[g * 7 + i] for i in range(7)], axis=1) for ref in (high_b, low_b)]
        chi[...] += dot3(d, b, (((1,), (1,)), ((), ())))

    def x_copy(step):
        there = (x + step) % NX
        return remote(
            chi.at[pl.ds(pl.multiple_of(there * BS, BS), BS)], rx.at[step - 1],
            x_send.at[step - 1], x_recv.at[step - 1], there * NZ + z, a,
        )

    for step in range(1, NX):
        x_copy(step).start()
    for step in range(1, NX):
        x_copy(step).wait()
    part = chi[pl.ds(pl.multiple_of(x * BS, BS), BS), :] + rx[0] + rx[1] + rx[2]
    turned = part.T
    zb[...] = jnp.concatenate([turned[: 2 * BS], turned[2 * BS :]], axis=1).reshape(NZ, 8, 2 * BS)

    def z_copy(step):
        there = (z + step) % NZ
        return remote(
            zb.at[there], rz.at[step - 1], z_send.at[step - 1], z_recv.at[step - 1], x * NZ + there, a
        )

    @pl.loop(1, NZ)
    def _(step):
        z_copy(step).start()

    @pl.loop(1, NZ)
    def _(step):
        z_copy(step).wait()

    total = zb[z]
    for i in range(NZ - 1):
        total = total + rz[i]
    fs[0] = total
    fs[1] = pltpu.roll(total, BS, 1)

    def f_copy(i):
        orb, aux, _ = targets[i]
        return remote(fs.at[i], rf.at[c], f_send.at[i], f_recv.at[c], orb, aux)

    for i in range(2):
        mine = targets[i][2]

        @pl.when(mine)
        def _():
            rf[c] = fs[i]

        @pl.when(jnp.logical_not(mine))
        def _():
            f_copy(i).start()

    for cs in range(2):

        @pl.when(jnp.logical_not(sources[cs][2]))
        def _():
            remote(fs.at[0], rf.at[cs], f_send.at[0], f_recv.at[cs], o, y * 2 + 1 - c).wait_recv()

    for i in range(2):

        @pl.when(jnp.logical_not(targets[i][2]))
        def _():
            f_copy(i).wait_send()

    out[...] = (rf[0] + rf[1])[:, :BS] * scale


def local(three_centre, green_occ, green_virt, owned_counts, pattern):
    lanes = three_centre.shape[3]
    chunks = lanes // CL
    aux_local = lanes // BS
    vmem, dma = pltpu.VMEM, pltpu.SemaphoreType.DMA
    smem = pl.BlockSpec(memory_space=pltpu.SMEM)
    block = pl.BlockSpec(memory_space=pltpu.VMEM)
    made = pl.pallas_call(
        functools.partial(kernel, 1.0 / math.sqrt(3 * NB * BS * BS)),
        out_shape=jax.ShapeDtypeStruct((8, BS), F32),
        in_specs=[block, block, block, smem, smem],
        out_specs=block,
        scratch_shapes=[
            vmem((2, 2, BS, 2 * BS), F32),
            vmem((2, 2, BS, 2 * BS), F32),
            vmem((BS // 2, 2 * BS), F32),
            vmem((2, BS, lanes), F32),
            vmem((2, BS, lanes), F32),
            vmem((2, BS, lanes), F32),
            vmem((2, BS, lanes), F32),
            vmem((2, BS, BS), F32),
            vmem((2, BS, BS), F32),
            vmem((3, BS, BS), F32),
            vmem((3, BS, BS), F32),
            vmem((NK, aux_local, 2 * BS), F32),
            vmem((NK, aux_local, 2 * BS), F32),
            vmem((HK, 4 * aux_local, 2 * BS), F32),
            vmem((HK, 4 * aux_local, 2 * BS), F32),
            vmem((3, CP * BS // 2, 2 * BS), F32),
            vmem((CP, 2 * BS), F32),
            vmem((HK, 4 * aux_local, 2 * BS), BF16),
            vmem((HK, 4 * aux_local, 2 * BS), BF16),
            vmem((2, 2, 5 * BS, 4 * BS), BF16),
            vmem((2, 2, 4 * BS, 4 * BS), BF16),
            vmem((2, 2, 10 * BS, 2 * BS), BF16),
            vmem((2, 2, 10 * BS, 2 * BS), BF16),
            vmem((4 * aux_local, 4 * aux_local), F32),
            vmem((NX - 1, aux_local, 4 * aux_local), F32),
            vmem((NZ, 8, 2 * BS), F32),
            vmem((NZ - 1, 8, 2 * BS), F32),
            vmem((2, 8, 2 * BS), F32),
            vmem((2, 8, 2 * BS), F32),
            dma((3, chunks)),
            dma((3, chunks)),
            dma((2,)),
            dma((2,)),
            dma((2, 3, chunks)),
            dma((2, 3, chunks)),
            dma((2, chunks)),
            dma((NX - 1,)),
            dma((NX - 1,)),
            dma((NZ - 1,)),
            dma((NZ - 1,)),
            dma((2,)),
            dma((2,)),
        ],
        compiler_params=pltpu.CompilerParams(
            collective_id=0, has_side_effects=True, vmem_limit_bytes=56 * 2**20
        ),
    )(
        three_centre,
        green_occ,
        green_virt,
        owned_counts,
        pattern,
    )
    return made.T


def solution(mesh):
    placed = (
        P("orb", None, None, "aux"),
        P("orb", None, None),
        P("orb", None, None),
        P(),
        P("orb", None),
    )
    return jax.shard_map(
        local, mesh=mesh, in_specs=placed, out_specs=P("aux", "orb"), check_vma=False
    )
```
